32 devices in a mesh: rep: 8 (over z, core), exp: 4 (over y, x).
Axes of the slice: x: 2, y: 2, z: 4, core: 2. Of those that a mesh axis runs over, the one named last changes fastest.
Arguments:
- tokens: bfloat16 [512, 2048], P('exp'), may hold values from -6 to 6
- expert_ids: int32 [512, 2], P('exp'), may hold values from 0 to 3, all different within a row; in each aligned block of 128 rows (0 to 127, 128 to 255, ...) at most 128 rows name the same one
- gate_values: float32 [512, 2], P('exp'), may hold values from 0.2 to 1
- grad_out: bfloat16 [512, 2048], P('exp'), may hold values from -6 to 6
- w_up: bfloat16 [4, 2048, 8192], P('exp', None, 'rep'), may hold values from -0.125 to 0.125
- w_down: bfloat16 [4, 8192, 2048], P('exp', 'rep'), may hold values from -0.0625 to 0.0625
Outputs:
- mixed: bfloat16 [512, 2048], P('exp', 'rep')
- grad_tokens: bfloat16 [512, 2048], P('exp', 'rep')
- grad_w_up: bfloat16 [4, 2048, 8192], P('exp', None, 'rep')
- grad_w_down: bfloat16 [4, 8192, 2048], P('exp', 'rep')
The draws below stay inside these ranges and needn't reach their ends.
Inputs may be any that keep to these rules, and one draw needn't show every extreme that they name: `expert_ids`: each row names 2 different experts. Within the rows of one index of exp (aligned blocks of 128 rows) no expert is named by more than 128 rows, a bound that some block reaches.
All inputs are finite; a program needn't handle non-finite values.
Results may differ from the reference program's by a relative error of at most 0.022.
Values may be sent and summed in bfloat16 or wider, within the bound.
A program may use at most 128 MiB of HBM per device.

```python
import math
import jax
import jax.numpy as jnp
import numpy as np
from jax import lax

D = 2048
FF = 8192
TOP = 2
TOK_DEV = 128
EXPERTS = 4
EXPERT_SLOTS = 128
TOKENS = 512
N_REP = 8
N_EXP = 4


def shard_levels(stream_key, extent, cuts, low, top_value):
    def one(axis_at, blocks):
        heights = jax.random.uniform(jax.random.fold_in(jax.random.fold_in(stream_key, 6), axis_at), (blocks,), jnp.float32, low / len(cuts), top_value / len(cuts))
        return jnp.repeat(jnp.exp(heights), extent[axis_at] // blocks).reshape((-1,) + (1,) * (len(extent) - axis_at - 1))

    loudness = one(*cuts[0])
    for cut in cuts[1:]:
        loudness = loudness * one(*cut)
    return loudness


def deal_out(rng, own, number, rows, amount, top, limit, lean):
    ranking = jax.random.permutation(rng, amount)
    packed, usual = shares(amount, rows * top, limit, lean, True), shares(amount, rows * top, limit, lean, False)
    places = jnp.arange(amount)

    def named(lengths, turn):
        used = int((lengths > 0).sum())
        fixed = max(1, used // 4)
        passed = fixed + (places - fixed + turn * (used - fixed)) % max(1, amount - fixed)
        return jnp.zeros((amount,), jnp.int32).at[ranking[jnp.where(places < fixed, places, passed)]].set(jnp.asarray(lengths, jnp.int32))

    lengths = jnp.where(number % 4 == 0, named(packed, number // 4), named(usual, number - number // 4 - 1))
    mixed = jax.random.permutation(jax.random.fold_in(own, 3), amount)
    giver, sink = mixed[0:amount // 2 * 2:2], mixed[1:amount // 2 * 2:2]
    margin = jnp.minimum(lengths[giver] - 1, limit - lengths[sink]) // 2
    margin = jnp.where((giver == ranking[0]) | (sink == ranking[0]) | (lengths[sink] == 0), 0, jnp.maximum(margin, 0))
    passed = jax.random.randint(jax.random.fold_in(own, 4), (amount // 2,), 0, 1 << 20) % (margin + 1)
    lengths = lengths.at[giver].add(-passed).at[sink].add(passed)
    items = jnp.searchsorted(jnp.cumsum(lengths), jnp.arange(rows * top), side="right").astype(jnp.int32)
    table = items.reshape(top, rows).T
    table = table[jax.random.permutation(jax.random.fold_in(own, 1), rows)]
    turn = jax.random.randint(jax.random.fold_in(own, 2), (rows, 1), 0, top)
    return jnp.take_along_axis(table, (jnp.arange(top)[None, :] + turn) % top, axis=1)


def shares(number_of, total, limit, skew, full):
    loads = [(1 << 20) // math.isqrt(grade ** skew) + 1 for grade in range(1, number_of + 1)]
    largest = limit if full else min(limit, max(-(-total // number_of), total * loads[0] // sum(loads)))
    least = 1 if total - largest >= number_of - 1 else 0
    given, surplus = [largest] + [least] * (number_of - 1), total - largest - least * (number_of - 1)
    while surplus > 0:
        candidates = [i for i in range(1, number_of) if given[i] < largest] or [i for i in range(1, number_of) if given[i] < limit]
        whole, left = sum([loads[i] for i in candidates]), surplus
        for i in candidates:
            more = min(limit - given[i], max(1, left * loads[i] // whole), surplus)
            given[i] = given[i] + more
            surplus = surplus - more
    return np.array(given)


def bell_draw(own_key, shape, width, reach, split=(), held_as=jnp.bfloat16):
    drawn = width * jax.random.normal(own_key, shape, jnp.float32)
    if split:
        drawn = drawn * shard_levels(own_key, shape, split, -0.22, 0.18)
    return jnp.clip(drawn, -reach, reach).astype(held_as)


def setup_inputs(seed: int = 0) -> dict:
    seeds = jax.random.split(jax.random.key(seed), 7)
    tokens = bell_draw(seeds[0], (TOKENS, D), 1.0, 6.0, ((0, 4),))
    expert_ids_keys = jax.random.split(jax.random.fold_in(seeds[1], 1), TOKENS // TOK_DEV)
    expert_ids_turns = jax.random.permutation(jax.random.fold_in(seeds[1], 3), TOKENS // TOK_DEV)
    expert_ids = jax.vmap(lambda own, number: deal_out(jax.random.fold_in(seeds[1], 2), own, number, TOK_DEV, EXPERTS, TOP, EXPERT_SLOTS, 1))(expert_ids_keys, expert_ids_turns).reshape((TOKENS, TOP))
    gate_values = jnp.clip(0.2 + 0.8 * jax.random.uniform(seeds[2], (TOKENS, TOP), jnp.float32) ** shard_levels(seeds[2], (TOKENS, TOP), ((0, 4),), -0.2, 0.2), 0.2, 1.0)
    grad_out = bell_draw(seeds[3], (TOKENS, D), 1.0, 6.0, ((0, 4),))
    w_up = bell_draw(seeds[4], (EXPERTS, D, FF), D ** -0.5, 0.125, ((0, 4), (2, 8)))
    w_down = bell_draw(seeds[5], (EXPERTS, FF, D), FF ** -0.5, 0.0625, ((0, 4), (1, 8)))
    return {"tokens": tokens, "expert_ids": expert_ids, "gate_values": gate_values, "grad_out": grad_out, "w_up": w_up, "w_down": w_down}


def silu_parts(preact):
    sigmoid_val = jax.nn.sigmoid(preact)
    return preact * sigmoid_val, sigmoid_val * (1.0 + preact * (1.0 - sigmoid_val))


def reference(tokens, expert_ids, gate_values, grad_out, w_up, w_down):
    device_total = N_EXP
    pair_count = TOK_DEV * TOP
    group_span_width = FF // N_REP
    expert_grid = expert_ids.reshape(device_total, pair_count)
    onehot = (expert_grid[:, :, None] == jnp.arange(EXPERTS, dtype=jnp.int32)[None, None, :]).astype(jnp.int32)
    before = jnp.cumsum(onehot, axis=1) - onehot
    position = jnp.sum(before * onehot, axis=2)
    device_ids = jnp.arange(device_total, dtype=jnp.int32)[:, None]
    slotting_labels = (device_ids * EXPERT_SLOTS + position).reshape(-1).astype(jnp.int32)
    flattened_experts = expert_grid.reshape(-1)
    pairing_total = device_total * pair_count
    slotting_total = device_total * EXPERT_SLOTS
    grad_rows = (gate_values[:, :, None] * grad_out[:, None, :].astype(jnp.float32)).astype(jnp.bfloat16)
    grad_rows = grad_rows.reshape(pairing_total, D)
    pairing_labels = jnp.arange(pairing_total, dtype=jnp.int32)

    def one_expert(expert_choice):
        destination = jnp.where(flattened_experts == expert_choice, slotting_labels, slotting_total).astype(jnp.int32)
        slotting_lookup = jnp.full((slotting_total,), pairing_total, dtype=jnp.int32).at[destination].set(pairing_labels, mode="drop")
        live_rows = slotting_lookup < pairing_total
        safe_rows = jnp.minimum(slotting_lookup, pairing_total - 1)
        zero_value = jnp.zeros((), jnp.bfloat16)
        rows_in = jnp.where(live_rows[:, None], tokens[safe_rows // TOP], zero_value)
        rows_grad = jnp.where(live_rows[:, None], grad_rows[safe_rows], zero_value)
        up_weight = w_up[expert_choice]
        down_weight = w_down[expert_choice]
        preact = jnp.dot(rows_in, up_weight, preferred_element_type=jnp.float32)
        value, slope = silu_parts(preact)
        hidden_units = value.astype(jnp.bfloat16)
        output_pieces = jnp.einsum("hkj,kjt->kht", hidden_units.reshape(slotting_total, N_REP, group_span_width).astype(jnp.float32),
                               down_weight.reshape(N_REP, group_span_width, D).astype(jnp.float32))
        output_pieces = lax.optimization_barrier(output_pieces.astype(jnp.bfloat16))
        out_row = jnp.sum(output_pieces.astype(jnp.float32), axis=0).astype(jnp.bfloat16)
        grad_hidden = jnp.dot(rows_grad, down_weight.T, preferred_element_type=jnp.float32)
        gradient_before_activation = (grad_hidden * slope).astype(jnp.bfloat16)
        grad_down_e = jnp.dot(hidden_units.T, rows_grad, preferred_element_type=jnp.float32).astype(jnp.bfloat16)
        grad_up_e = jnp.dot(rows_in.T, gradient_before_activation, preferred_element_type=jnp.float32).astype(jnp.bfloat16)
        input_grad_pieces = jnp.einsum("pbx,cbx->bpc", gradient_before_activation.reshape(slotting_total, N_REP, group_span_width).astype(jnp.float32),
                              up_weight.reshape(D, N_REP, group_span_width).astype(jnp.float32))
        input_grad_pieces = lax.optimization_barrier(input_grad_pieces.astype(jnp.bfloat16))
        dx_row = jnp.sum(input_grad_pieces.astype(jnp.float32), axis=0).astype(jnp.bfloat16)
        return out_row, dx_row, grad_up_e, grad_down_e

    out_rows, dx_rows, grad_w_up, grad_w_down = lax.map(one_expert, jnp.arange(EXPERTS, dtype=jnp.int32))
    pairing_index = (flattened_experts * slotting_total + slotting_labels).astype(jnp.int32)
    out_pairs = out_rows.reshape(-1, D)[pairing_index].astype(jnp.float32).reshape(TOKENS, TOP, D)
    mixed = jnp.sum(gate_values[:, :, None] * out_pairs, axis=1).astype(jnp.bfloat16)
    dx_pairs = dx_rows.reshape(-1, D)[pairing_index].astype(jnp.float32).reshape(TOKENS, TOP, D)
    grad_tokens = jnp.sum(dx_pairs, axis=1).astype(jnp.bfloat16)
    return mixed, grad_tokens, grad_w_up, grad_w_down
```

```python
import functools

import jax
import jax.numpy as jnp
from jax import lax
from jax.experimental import pallas as pl
from jax.experimental.pallas import tpu as pltpu
from jax.sharding import PartitionSpec as P

MESH = pl.DeviceIdType.MESH
F32 = jnp.float32
BF16 = jnp.bfloat16
NN = (((1,), (0,)), ((), ()))
NT = (((1,), (1,)), ((), ()))
TN = (((0,), (0,)), ((), ()))


def dot(a, b, dims):
    return lax.dot_general(a, b, dims, preferred_element_type=F32)


def fused_kernel(
    weight_in, tok, gout, up_hbm, down_hbm,
    mixed_out, gtok_out, gup_hbm, gdown_hbm,
    x_all, g_all, gr_all, weight_all, coef, up, down, slope, hid, gpre,
    send_a, recv_a, s_sum, recv_1, mid, recv_2, q_sum, recv_3, gup, gdown,
    load_sem, meta_send, meta_recv, gat_send, gat_recv,
    a_send, a_recv, b_send, b_recv, t_send, t_recv, c_send, c_recv, gup_sem, gdown_sem,
):
    rep, e = lax.axis_index("rep"), lax.axis_index("exp")
    z, c = lax.div(rep, 2), lax.rem(rep, 2)
    y, x = lax.div(e, 2), lax.rem(e, 2)
    xn, yn = 1 - x, 1 - y
    ex, ey, ed = y * 2 + xn, yn * 2 + x, yn * 2 + xn
    p = lax.rem(z, 2)
    to_x = {"rep": rep, "exp": ex}
    to_y = {"rep": rep, "exp": ey}
    to_d = {"rep": rep, "exp": ed}
    to_sib = {"rep": z * 2 + 1 - c, "exp": e}
    to_pair = {"rep": (z + 1 - 2 * p) * 2 + c, "exp": e}

    def at_z(d):
        zz = lax.rem(z + d, 4)
        return zz, {"rep": zz * 2 + c, "exp": e}

    def remote(src, dst, send, recv, where):
        return pltpu.make_async_remote_copy(
            src_ref=src, dst_ref=dst, send_sem=send, recv_sem=recv,
            device_id=where, device_id_type=MESH,
        )

    load_up = pltpu.make_async_copy(up_hbm, up, load_sem.at[0])
    load_down = pltpu.make_async_copy(down_hbm, down, load_sem.at[1])
    load_up.start()
    load_down.start()

    barrier = pltpu.get_barrier_semaphore()
    partners = [to_x, to_y, to_d, to_sib] + [at_z(d)[1] for d in (1, 2, 3)]
    for who in partners:
        pl.semaphore_signal(barrier, inc=1, device_id=who, device_id_type=MESH)
    pl.semaphore_wait(barrier, len(partners))

    lo, own_rows, mid_rows, pair_rows = 64 * c + 16 * p, 64 * c + 48 * p, 64 * c + 16, 64 * c + 48 - 48 * p

    def rows(block, start, count):
        return pl.ds(pl.multiple_of(block * 128 + start, 16), count)

    class Gather:
        def __init__(self, t, own, buf):
            self.t, self.own, self.buf, self.copies = t, own, buf, {}

        def send(self, k, src, block, start, count, where):
            at = rows(block, start, count)
            copy = remote(
                self.buf.at[at] if src is None else src, self.buf.at[at],
                gat_send.at[self.t, k], gat_recv.at[self.t, k], where,
            )
            copy.start()
            self.copies[k] = copy

        def direct(self):
            mine = self.own.at[pl.ds(pl.multiple_of(lo, 16), 48)]
            self.send(0, mine, e, lo, 48, to_x)
            self.send(1, mine, e, lo, 48, to_y)

        def keep(self):
            self.buf[rows(e, 0, 128), :] = self.own[...]

        def forward(self):
            first = (own_rows, 16) if self.t == 0 else (mid_rows, 32)
            second = (mid_rows, 32) if self.t == 0 else (own_rows, 16)
            self.copies[0].wait_recv()
            self.send(2, None, ex, *first, to_y)
            self.send(4, None, ex, own_rows, 16, to_pair)
            self.send(7, None, ex, lo, 48, to_sib)
            self.copies[1].wait_recv()
            self.send(3, None, ey, *second, to_x)
            self.send(5, None, ey, own_rows, 16, to_pair)
            self.send(8, None, ey, lo, 48, to_sib)

        def diagonal(self):
            self.copies[2].wait_recv()
            self.copies[3].wait_recv()
            self.send(6, None, ed, own_rows, 16, to_pair)
            self.send(9, None, ed, lo, 48, to_sib)

        def pair(self):
            for k, block in ((4, ex), (5, ey), (6, ed)):
                self.copies[k].wait_recv()
                self.send(6 + k, None, block, pair_rows, 16, to_sib)

        def finish(self):
            for k in range(7, 13):
                self.copies[k].wait_recv()

        def drain(self):
            for k in range(13):
                self.copies[k].wait_send()

    gx, gg = Gather(0, tok, x_all), Gather(1, gout, g_all)
    gx.direct()
    weights = []
    for k, where in enumerate((to_x, to_y, to_d)):
        copy = remote(weight_in, weight_all.at[e], meta_send.at[k], meta_recv.at[k], where)
        copy.start()
        weights.append(copy)
    gx.keep()
    gg.keep()
    weight_all[pl.ds(e, 1)] = weight_in[...][None]
    for copy in weights:
        copy.wait_recv()
    for block in range(4):
        line = weight_all[block, pl.ds(e, 1), :]
        coef[128 * block : 128 * block + 128, :] = jnp.broadcast_to(line, (128, 128)).T
    gx.forward()
    gg.direct()
    gx.diagonal()
    gx.pair()
    load_up.wait()
    gx.finish()

    def cols(n):
        return pl.ds(pl.multiple_of(n * 256, 256), 256)

    def up_tile(n, carry):
        pre = dot(x_all[...], up[:, cols(n)], NN)
        sig = jax.nn.sigmoid(pre)
        hid[:, cols(n)] = (pre * sig).astype(BF16)
        slope[:, cols(n)] = sig * (1.0 + pre * (1.0 - sig))
        return carry

    lax.fori_loop(0, 2, up_tile, 0)
    gg.forward()
    lax.fori_loop(2, 4, up_tile, 0)
    load_down.wait()

    def partial(q, n):
        if q == 0:
            scale = coef[...]
            return dot(hid[...], down[:, cols(n)], NN) * jnp.concatenate([scale, scale], axis=1)
        return dot(gpre[...], up[cols(n), :], NT)

    def copy_a(q, zz):
        return remote(send_a.at[q, zz], recv_a.at[q, zz], a_send.at[q, zz], a_recv.at[q, zz], to_sib)

    def copy_b(q, zz, x_first):
        src = s_sum.at[q, zz, :, xn] if x_first else s_sum.at[q, zz, yn]
        where = to_x if x_first else to_y
        return remote(src, recv_1.at[q, zz], b_send.at[q, zz], b_recv.at[q, zz], where)

    def copy_t(q, zz, x_first):
        where = to_y if x_first else to_x
        return remote(mid.at[q, zz], recv_2.at[q, zz], t_send.at[q, zz], t_recv.at[q, zz], where)

    def copy_c(q, d):
        zz, where = at_z(d)
        return remote(q_sum.at[q, zz], recv_3.at[q, d - 1], c_send.at[q, d - 1], c_recv.at[q, d - 1], where)

    def other_half(q):
        def body(zz, carry):
            send_a[q, zz] = partial(q, 2 * zz + 1 - c).astype(BF16)
            copy_a(q, zz).start()
            return carry
        lax.fori_loop(0, 4, body, 0)

    def own_half(q):
        def body(x_first, zz, carry):
            part = partial(q, 2 * zz + c)
            copy_a(q, zz).wait_recv()
            total = (part + recv_a[q, zz].astype(F32)).astype(BF16)
            s_sum[q, zz] = total.reshape(2, 2, 128, 256)
            copy_b(q, zz, x_first).start()
            return carry
        lax.fori_loop(0, 2, functools.partial(body, True), 0)
        lax.fori_loop(2, 4, functools.partial(body, False), 0)

    def second_hop(q):
        for zz in (0, 2, 1, 3):
            x_first = zz < 2
            copy_b(q, zz, x_first).wait_recv()
            mine = s_sum[q, zz, yn, x] if x_first else s_sum[q, zz, y, xn]
            got = recv_1[q, zz, yn] if x_first else recv_1[q, zz, xn]
            mid[q, zz] = (mine.astype(F32) + got.astype(F32)).astype(BF16)
            copy_t(q, zz, x_first).start()

    def along_z(q):
        for zz in (0, 2, 1, 3):
            x_first = zz < 2
            copy_t(q, zz, x_first).wait_recv()
            got = recv_1[q, zz, y] if x_first else recv_1[q, zz, x]
            total = s_sum[q, zz, y, x].astype(F32) + got.astype(F32) + recv_2[q, zz].astype(F32)
            q_sum[q, zz] = total.astype(BF16)
        for d in (2, 1, 3):
            copy_c(q, d).start()

    def result(q, out):
        total = q_sum[q, z].astype(F32)
        for d in (1, 2, 3):
            copy_c(q, d).wait_recv()
            total = total + recv_3[q, d - 1].astype(F32)
        out[...] = total.astype(BF16)

    def gup_tile(n, carry):
        gup[cols(n), :] = dot(x_all[:, cols(n)], gpre[...], TN).astype(BF16)
        pltpu.make_async_copy(gup.at[cols(n)], gup_hbm.at[cols(n)], gup_sem.at[n]).start()
        return carry

    def gdown_tile(n, carry):
        gdown[cols(n), :] = dot(hid[:, cols(n)], gr_all[...], TN).astype(BF16)
        pltpu.make_async_copy(gdown.at[cols(n)], gdown_hbm.at[cols(n)], gdown_sem.at[n]).start()
        return carry

    other_half(0)
    gg.diagonal()
    gg.pair()
    own_half(0)
    gg.finish()

    def scale_tile(n, carry):
        at = pl.ds(pl.multiple_of(n * 128, 128), 128)
        gr_all[:, at] = (g_all[:, at].astype(F32) * coef[...]).astype(BF16)
        return carry

    lax.fori_loop(0, 16, scale_tile, 0)

    def gpre_tile(n, carry):
        gpre[:, cols(n)] = (dot(gr_all[...], down[cols(n), :], NT) * slope[:, cols(n)]).astype(BF16)
        return carry

    lax.fori_loop(0, 4, gpre_tile, 0)
    second_hop(0)
    other_half(1)
    own_half(1)
    along_z(0)
    lax.fori_loop(0, 4, gdown_tile, 0)
    second_hop(1)
    lax.fori_loop(0, 4, gup_tile, 0)
    along_z(1)
    lax.fori_loop(4, 8, gup_tile, 0)
    result(0, mixed_out)
    result(1, gtok_out)

    gx.drain()
    gg.drain()
    for copy in weights:
        copy.wait_send()
    for q in (0, 1):
        for zz in range(4):
            copy_a(q, zz).wait_send()
            copy_b(q, zz, zz < 2).wait_send()
            copy_t(q, zz, zz < 2).wait_send()
        for d in (1, 2, 3):
            copy_c(q, d).wait_send()
    for n in range(8):
        pltpu.make_async_copy(gup.at[cols(n)], gup_hbm.at[cols(n)], gup_sem.at[n]).wait()
    for n in range(4):
        pltpu.make_async_copy(gdown.at[cols(n)], gdown_hbm.at[cols(n)], gdown_sem.at[n]).wait()


def fused(tokens, expert_ids, gate_values, grad_out, w_up, w_down):
    experts = jnp.arange(8, dtype=jnp.int32)[:, None, None]
    weight = jnp.sum(jnp.where(expert_ids.T[None] == experts, gate_values.T[None], 0.0), axis=1)
    up, down = w_up[0], w_down[0]
    width, units = up.shape
    vmem, dma = pltpu.VMEM, pltpu.SemaphoreType.DMA
    whole, anywhere = pl.BlockSpec(memory_space=pltpu.VMEM), pl.BlockSpec(memory_space=pl.ANY)
    small = jax.ShapeDtypeStruct((128, 256), BF16)
    mixed, gtok, gup, gdown = pl.pallas_call(
        fused_kernel,
        out_shape=(
            small, small,
            jax.ShapeDtypeStruct((width, units), BF16),
            jax.ShapeDtypeStruct((units, width), BF16),
        ),
        in_specs=[whole] * 3 + [anywhere] * 2,
        out_specs=(whole, whole, anywhere, anywhere),
        scratch_shapes=[
            vmem((512, width), BF16), vmem((512, width), BF16), vmem((512, width), BF16),
            vmem((4, 8, 128), F32), vmem((512, 128), F32),
            vmem((width, units), BF16), vmem((units, width), BF16),
            vmem((512, units), F32), vmem((512, units), BF16), vmem((512, units), BF16),
            vmem((2, 4, 512, 256), BF16), vmem((2, 4, 512, 256), BF16),
            vmem((2, 4, 2, 2, 128, 256), BF16), vmem((2, 4, 2, 128, 256), BF16),
            vmem((2, 4, 128, 256), BF16), vmem((2, 4, 128, 256), BF16),
            vmem((2, 4, 128, 256), BF16), vmem((2, 3, 128, 256), BF16),
            vmem((width, units), BF16), vmem((units, width), BF16),
            dma((2,)), dma((3,)), dma((3,)), dma((2, 13)), dma((2, 13)),
            dma((2, 4)), dma((2, 4)), dma((2, 4)), dma((2, 4)), dma((2, 4)), dma((2, 4)),
            dma((2, 3)), dma((2, 3)), dma((8,)), dma((4,)),
        ],
        compiler_params=pltpu.CompilerParams(
            collective_id=0, has_side_effects=True, vmem_limit_bytes=56 * 1024 * 1024
        ),
        cost_estimate=pl.CostEstimate(flops=12 * 512 * width * units, bytes_accessed=8 * width * units, transcendentals=512 * units),
    )(weight, tokens, grad_out, up, down)
    return mixed, gtok, gup[None], gdown[None]


def plan_slots(routed, experts, capacity):
    flat_ids = routed.reshape(-1)
    onehot = (flat_ids[:, None] == jnp.arange(experts, dtype=jnp.int32)[None, :]).astype(jnp.int32)
    before = jnp.cumsum(onehot, axis=0) - onehot
    position = jnp.sum(before * onehot, axis=1)
    counts = jnp.sum(onehot, axis=0)
    slotting_labels = flat_ids * capacity + position
    placed = (
        slotting_labels[None, :] == jnp.arange(experts * capacity, dtype=jnp.int32)[:, None]
    ).astype(jnp.bfloat16)
    return (placed, counts)


def expert_math(rows_in, rows_grad, live_mask, up_weight, down_weight):
    preact = jnp.dot(rows_in, up_weight, preferred_element_type=jnp.float32)
    sigmoid_val = jax.nn.sigmoid(preact)
    keep = live_mask[:, None]
    hidden_units = jnp.where(keep, preact * sigmoid_val, 0.0).astype(jnp.bfloat16)
    out_part = jnp.dot(hidden_units, down_weight, preferred_element_type=jnp.float32)
    grad_hidden = lax.dot_general(
        rows_grad, down_weight, (((1,), (1,)), ((), ())), preferred_element_type=jnp.float32
    )
    slope = sigmoid_val * (1.0 + preact * (1.0 - sigmoid_val))
    gradient_before_activation = jnp.where(keep, grad_hidden * slope, 0.0).astype(jnp.bfloat16)
    grad_down_e = lax.dot_general(
        hidden_units, rows_grad, (((0,), (0,)), ((), ())), preferred_element_type=jnp.float32
    )
    grad_up_e = lax.dot_general(
        rows_in,
        gradient_before_activation,
        (((0,), (0,)), ((), ())),
        preferred_element_type=jnp.float32,
    )
    dx_part = lax.dot_general(
        gradient_before_activation,
        up_weight,
        (((1,), (1,)), ((), ())),
        preferred_element_type=jnp.float32,
    )
    return (out_part, dx_part, grad_up_e, grad_down_e)


def local(tokens, expert_ids, gate_values, grad_out, w_up, w_down):
    n_rep = lax.axis_size("rep")
    n_exp = lax.axis_size("exp")
    if (n_rep, n_exp) == (8, 4) and tokens.shape == (128, 2048) and w_up.shape[2] == 1024:
        return fused(tokens, expert_ids, gate_values, grad_out, w_up, w_down)
    tok_count, width = tokens.shape
    top_k = expert_ids.shape[1]
    pair_count = tok_count * top_k
    capacity = max(2, min(tok_count, 2 * tok_count * top_k // n_exp))
    cols = width // n_rep
    up_weight = w_up[0]
    down_weight = w_down[0]
    grad_rows = (gate_values[:, :, None] * grad_out[:, None, :].astype(jnp.float32)).astype(
        jnp.bfloat16
    )
    grad_rows = grad_rows.reshape(pair_count, width)
    placed, counts = plan_slots(expert_ids, n_exp, capacity)
    summed = placed.reshape(n_exp * capacity, tok_count, top_k).sum(axis=2)
    sent_in = jnp.dot(summed, tokens, preferred_element_type=jnp.float32).astype(jnp.bfloat16)
    sent_grad = jnp.dot(placed, grad_rows, preferred_element_type=jnp.float32).astype(jnp.bfloat16)
    count_parts = jnp.stack([counts // 16, counts % 16], axis=1).astype(jnp.bfloat16)
    got_in, got_grad, got_counts = (
        lax.all_to_all(
            sent_in.reshape(n_exp, capacity, width), "exp", split_axis=0, concat_axis=0, tiled=True
        ),
        lax.all_to_all(
            sent_grad.reshape(n_exp, capacity, width),
            "exp",
            split_axis=0,
            concat_axis=0,
            tiled=True,
        ),
        lax.all_to_all(count_parts, "exp", split_axis=0, concat_axis=0, tiled=True),
    )
    count_values = got_counts[:, 0].astype(jnp.float32) * 16.0 + got_counts[:, 1].astype(
        jnp.float32
    )
    slot_mask = jnp.arange(capacity, dtype=jnp.float32)[None, :] < count_values[:, None]
    rows_in = got_in.reshape(-1, width)
    rows_grad = got_grad.reshape(-1, width)
    live_mask = slot_mask.reshape(-1)
    out_part, dx_part, grad_up_e, grad_down_e = expert_math(
        rows_in, rows_grad, live_mask, up_weight, down_weight
    )
    total_out, total_dx = (
        lax.psum(out_part.astype(jnp.bfloat16), "rep").astype(jnp.float32),
        lax.psum(dx_part.astype(jnp.bfloat16), "rep").astype(jnp.float32),
    )
    col_start = lax.axis_index("rep") * cols
    summed_out = lax.dynamic_slice_in_dim(total_out, col_start, cols, 1)
    summed_dx = lax.dynamic_slice_in_dim(total_dx, col_start, cols, 1)
    back_out, back_dx = (
        lax.all_to_all(
            summed_out.astype(jnp.bfloat16).reshape(n_exp, capacity, cols),
            "exp",
            split_axis=0,
            concat_axis=0,
            tiled=True,
        ),
        lax.all_to_all(
            summed_dx.astype(jnp.bfloat16).reshape(n_exp, capacity, cols),
            "exp",
            split_axis=0,
            concat_axis=0,
            tiled=True,
        ),
    )
    pair_out = jnp.einsum(
        "st,sd->td",
        placed,
        back_out.reshape(n_exp * capacity, cols),
        preferred_element_type=jnp.float32,
    )
    pair_dx = jnp.einsum(
        "st,sd->td",
        placed,
        back_dx.reshape(n_exp * capacity, cols),
        preferred_element_type=jnp.float32,
    )
    mixed = jnp.sum(gate_values[:, :, None] * pair_out.reshape(tok_count, top_k, cols), axis=1)
    grad_tokens = jnp.sum(pair_dx.reshape(tok_count, top_k, cols), axis=1)
    return (
        mixed.astype(jnp.bfloat16),
        grad_tokens.astype(jnp.bfloat16),
        grad_up_e.astype(jnp.bfloat16)[None],
        grad_down_e.astype(jnp.bfloat16)[None],
    )


def solution(mesh):
    return jax.shard_map(
        local,
        mesh=mesh,
        in_specs=(
            P("exp", None),
            P("exp", None),
            P("exp", None),
            P("exp", None),
            P("exp", None, "rep"),
            P("exp", "rep", None),
        ),
        out_specs=(P("exp", "rep"), P("exp", "rep"), P("exp", None, "rep"), P("exp", "rep", None)),
        check_vma=False,
    )
```

```python
import functools

import jax
import jax.numpy as jnp
from jax import lax
from jax.experimental import pallas as pl
from jax.experimental.pallas import tpu as pltpu
from jax.sharding import PartitionSpec as P

MESH = pl.DeviceIdType.MESH
F32 = jnp.float32
BF16 = jnp.bfloat16
NN = (((1,), (0,)), ((), ()))
NT = (((1,), (1,)), ((), ()))
TN = (((0,), (0,)), ((), ()))


def dot(a, b, dims):
    return lax.dot_general(a, b, dims, preferred_element_type=F32)


def fused_kernel(
    ids, gates, tok, gout, up_hbm, down_hbm,
    mixed_out, gtok_out, gup_hbm, gdown_hbm,
    x_all, g_all, gr_all, weight_all, coef, up, down, slope, hid, gpre,
    send_a, recv_a, s_sum, recv_1, mid, recv_2, q_sum, recv_3, gup, gdown,
    load_sem, meta_send, meta_recv, gat_send, gat_recv,
    a_send, a_recv, b_send, b_recv, t_send, t_recv, c_send, c_recv, gup_sem, gdown_sem,
):
    rep, e = lax.axis_index("rep"), lax.axis_index("exp")
    z, c = lax.div(rep, 2), lax.rem(rep, 2)
    y, x = lax.div(e, 2), lax.rem(e, 2)
    xn, yn = 1 - x, 1 - y
    ex, ey, ed = y * 2 + xn, yn * 2 + x, yn * 2 + xn
    p = lax.rem(z, 2)
    to_x = {"rep": rep, "exp": ex}
    to_y = {"rep": rep, "exp": ey}
    to_d = {"rep": rep, "exp": ed}
    to_sib = {"rep": z * 2 + 1 - c, "exp": e}
    to_pair = {"rep": (z + 1 - 2 * p) * 2 + c, "exp": e}

    def at_z(d):
        zz = lax.rem(z + d, 4)
        return zz, {"rep": zz * 2 + c, "exp": e}

    def remote(src, dst, send, recv, where):
        return pltpu.make_async_remote_copy(
            src_ref=src, dst_ref=dst, send_sem=send, recv_sem=recv,
            device_id=where, device_id_type=MESH,
        )

    load_up = pltpu.make_async_copy(up_hbm, up, load_sem.at[0])
    load_down = pltpu.make_async_copy(down_hbm, down, load_sem.at[1])
    load_up.start()
    load_down.start()

    barrier = pltpu.get_barrier_semaphore()
    partners = [to_x, to_y, to_d, to_sib] + [at_z(d)[1] for d in (1, 2, 3)]
    for who in partners:
        pl.semaphore_signal(barrier, inc=1, device_id=who, device_id_type=MESH)
    pl.semaphore_wait(barrier, len(partners))

    lo, own_rows, mid_rows, pair_rows = 64 * c + 16 * p, 64 * c + 48 * p, 64 * c + 16, 64 * c + 48 - 48 * p

    def rows(block, start, count):
        return pl.ds(pl.multiple_of(block * 128 + start, 16), count)

    class Gather:
        def __init__(self, t, own, buf):
            self.t, self.own, self.buf, self.copies = t, own, buf, {}

        def send(self, k, src, block, start, count, where):
            at = rows(block, start, count)
            copy = remote(
                self.buf.at[at] if src is None else src, self.buf.at[at],
                gat_send.at[self.t, k], gat_recv.at[self.t, k], where,
            )
            copy.start()
            self.copies[k] = copy

        def direct(self):
            own_piece, mid_piece = (own_rows, 16), (mid_rows, 32)
            self.pieces = (own_piece, mid_piece) if self.t == 0 else (mid_piece, own_piece)
            first, second = self.pieces
            for k, (start, count), where in ((0, first, to_x), (1, second, to_y), (2, second, to_x), (3, first, to_y)):
                mine = self.own.at[pl.ds(pl.multiple_of(start, 16), count)]
                self.send(k, mine, e, start, count, where)

        def keep(self):
            self.buf[rows(e, 0, 128), :] = self.own[...]

        def around(self):
            first, second = self.pieces
            self.copies[0].wait_recv()
            self.send(4, None, ex, *first, to_y)
            self.copies[1].wait_recv()
            self.send(5, None, ey, *second, to_x)

        def share(self):
            self.copies[2].wait_recv()
            self.send(6, None, ex, own_rows, 16, to_pair)
            self.send(9, None, ex, lo, 48, to_sib)
            self.copies[3].wait_recv()
            self.send(7, None, ey, own_rows, 16, to_pair)
            self.send(10, None, ey, lo, 48, to_sib)

        def diagonal(self):
            self.copies[4].wait_recv()
            self.copies[5].wait_recv()
            self.send(8, None, ed, own_rows, 16, to_pair)
            self.send(11, None, ed, lo, 48, to_sib)

        def pair(self):
            for k, block in ((6, ex), (7, ey), (8, ed)):
                self.copies[k].wait_recv()
                self.send(6 + k, None, block, pair_rows, 16, to_sib)

        def finish(self, blocks):
            for k in blocks:
                self.copies[9 + k].wait_recv()
                self.copies[12 + k].wait_recv()

        def drain(self):
            for k in range(15):
                self.copies[k].wait_send()

    gx, gg = Gather(0, tok, x_all), Gather(1, gout, g_all)
    gx.direct()
    expert = lax.broadcasted_iota(jnp.int32, (8, 128), 0)
    first_gate = jnp.where(ids[0:1, :] == expert, gates[0:1, :], 0.0)
    weight_all[pl.ds(e, 1)] = (first_gate + jnp.where(ids[1:2, :] == expert, gates[1:2, :], 0.0))[None]
    weights = []
    for k, where in enumerate((to_x, to_y, to_d)):
        copy = remote(weight_all.at[e], weight_all.at[e], meta_send.at[k], meta_recv.at[k], where)
        copy.start()
        weights.append(copy)
    gx.keep()
    gg.keep()
    gx.around()
    gg.direct()
    gx.share()
    for copy in weights:
        copy.wait_recv()
    for block in range(4):
        line = weight_all[block, pl.ds(e, 1), :]
        coef[128 * block : 128 * block + 128, :] = jnp.broadcast_to(line, (128, 128)).T
    gx.diagonal()
    gx.pair()
    load_up.wait()

    def cols(n):
        return pl.ds(pl.multiple_of(n * 256, 256), 256)

    def up_half(yy):
        for n in range(4):
            pre = dot(x_all[cols(yy), :], up[:, cols(n)], NN)
            sig = jax.nn.sigmoid(pre)
            hid[cols(yy), cols(n)] = (pre * sig).astype(BF16)
            slope[cols(yy), cols(n)] = sig * (1.0 + pre * (1.0 - sig))

    gx.finish((0,))
    up_half(y)
    gg.around()
    gx.finish((1, 2))
    up_half(yn)
    gg.share()
    load_down.wait()

    def partial(q, yy, n):
        if q == 0:
            scale = coef[cols(yy), :]
            return dot(hid[cols(yy), :], down[:, cols(n)], NN) * jnp.concatenate([scale, scale], axis=1)
        return dot(gpre[cols(yy), :], up[cols(n), :], NT)

    def copy_a(q, yy, zz):
        return remote(
            send_a.at[q, zz, yy], recv_a.at[q, zz, yy], a_send.at[q, zz, yy], a_recv.at[q, zz, yy], to_sib
        )

    def copy_bx(q, yy, zz):
        return remote(
            s_sum.at[q, zz, yy, xn], recv_1.at[q, zz, yy], b_send.at[q, zz, yy], b_recv.at[q, zz, yy], to_x
        )

    def copy_by(q, zz):
        return remote(s_sum.at[q, zz, yn], recv_1.at[q, zz], b_send.at[q, zz, 0], b_recv.at[q, zz, 0], to_y)

    def copy_t(q, zz):
        where = to_y if zz < 2 else to_x
        return remote(mid.at[q, zz], recv_2.at[q, zz], t_send.at[q, zz], t_recv.at[q, zz], where)

    def copy_c(q, zz, d):
        where = {"rep": zz * 2 + c, "exp": e}
        return remote(q_sum.at[q, zz], recv_3.at[q, d - 1], c_send.at[q, d - 1], c_recv.at[q, d - 1], where)

    def other_half(q, yy):
        def body(zz, carry):
            send_a[q, zz, yy] = partial(q, yy, 2 * zz + 1 - c).astype(BF16)
            copy_a(q, yy, zz).start()
            return carry
        lax.fori_loop(0, 4, body, 0)

    def own_half(q, yy, far):
        def body(x_first, zz, carry):
            part = partial(q, yy, 2 * zz + c)
            copy_a(q, yy, zz).wait_recv()
            total = (part + recv_a[q, zz, yy].astype(F32)).astype(BF16)
            s_sum[q, zz, yy] = total.reshape(2, 128, 256)
            if x_first:
                copy_bx(q, yy, zz).start()
            elif far:
                copy_by(q, zz).start()
            return carry
        lax.fori_loop(2, 4, functools.partial(body, False), 0)
        lax.fori_loop(0, 2, functools.partial(body, True), 0)

    def second_hop(q, zs):
        for zz in zs:
            if zz < 2:
                copy_bx(q, yn, zz).wait_recv()
                mine, got = s_sum[q, zz, yn, x], recv_1[q, zz, yn]
            else:
                copy_by(q, zz).wait_recv()
                mine, got = s_sum[q, zz, y, xn], recv_1[q, zz, xn]
            mid[q, zz] = (mine.astype(F32) + got.astype(F32)).astype(BF16)
            copy_t(q, zz).start()

    def along_z(q, zs):
        for zz in zs:
            if zz < 2:
                copy_bx(q, y, zz).wait_recv()
            copy_t(q, zz).wait_recv()
            got = recv_1[q, zz, y] if zz < 2 else recv_1[q, zz, x]
            total = s_sum[q, zz, y, x].astype(F32) + got.astype(F32) + recv_2[q, zz].astype(F32)
            q_sum[q, zz] = total.astype(BF16)
            d = lax.rem(zz - z + 4, 4)

            @pl.when(d > 0)
            def _():
                copy_c(q, zz, d).start()

    def result(q, out):
        total = q_sum[q, z].astype(F32)
        for d in (1, 2, 3):
            copy_c(q, lax.rem(z + d, 4), d).wait_recv()
            total = total + recv_3[q, d - 1].astype(F32)
        out[...] = total.astype(BF16)

    def gup_tile(n, carry):
        gup[cols(n), :] = dot(x_all[:, cols(n)], gpre[...], TN).astype(BF16)
        pltpu.make_async_copy(gup.at[cols(n)], gup_hbm.at[cols(n)], gup_sem.at[n]).start()
        return carry

    def gdown_tile(n, carry):
        gdown[cols(n), :] = dot(hid[:, cols(n)], gr_all[...], TN).astype(BF16)
        pltpu.make_async_copy(gdown.at[cols(n)], gdown_hbm.at[cols(n)], gdown_sem.at[n]).start()
        return carry

    other_half(0, y)
    gg.diagonal()
    own_half(0, y, False)
    other_half(0, yn)
    gg.pair()
    own_half(0, yn, True)
    gg.finish((0, 1, 2))

    def scale_half(yy):
        for n in range(16):
            at = pl.ds(n * 128, 128)
            gr_all[cols(yy), at] = (g_all[cols(yy), at].astype(F32) * coef[cols(yy), :]).astype(BF16)

    def gpre_half(yy):
        for n in range(4):
            grad = dot(gr_all[cols(yy), :], down[cols(n), :], NT)
            gpre[cols(yy), cols(n)] = (grad * slope[cols(yy), cols(n)]).astype(BF16)

    order = (2, 0, 3, 1)
    scale_half(yn)
    gpre_half(yn)
    second_hop(0, order)
    other_half(1, yn)
    own_half(1, yn, True)
    scale_half(y)
    gpre_half(y)
    along_z(0, order)
    other_half(1, y)
    second_hop(1, (0, 1))
    own_half(1, y, False)
    second_hop(1, (2, 3))
    lax.fori_loop(0, 4, gdown_tile, 0)
    along_z(1, (0, 2))
    lax.fori_loop(0, 1, gup_tile, 0)
    along_z(1, (1, 3))
    lax.fori_loop(1, 8, gup_tile, 0)
    result(0, mixed_out)
    result(1, gtok_out)

    gx.drain()
    gg.drain()
    for copy in weights:
        copy.wait_send()
    for q in (0, 1):
        for zz in range(4):
            for yy in (0, 1):
                copy_a(q, yy, zz).wait_send()
            if zz < 2:
                copy_bx(q, 0, zz).wait_send()
                copy_bx(q, 1, zz).wait_send()
            else:
                copy_by(q, zz).wait_send()
            copy_t(q, zz).wait_send()
        for d in (1, 2, 3):
            copy_c(q, lax.rem(z + d, 4), d).wait_send()
    for n in range(8):
        pltpu.make_async_copy(gup.at[cols(n)], gup_hbm.at[cols(n)], gup_sem.at[n]).wait()
    for n in range(4):
        pltpu.make_async_copy(gdown.at[cols(n)], gdown_hbm.at[cols(n)], gdown_sem.at[n]).wait()


def settle_kernel(mixed, gtok, gup, gdown, mixed_out, gtok_out, gup_out, gdown_out, sem):
    pieces = [(mixed, mixed_out), (gtok, gtok_out)]
    for src, dst in ((gup, gup_out), (gdown, gdown_out)):
        step = src.shape[0] // 8
        pieces += [(src.at[pl.ds(k * step, step)], dst.at[pl.ds(k * step, step)]) for k in range(8)]
    copies = [pltpu.make_async_copy(src, dst, sem.at[k]) for k, (src, dst) in enumerate(pieces)]
    for copy in copies:
        copy.start()
    for copy in copies:
        copy.wait()


def fused(tokens, expert_ids, gate_values, grad_out, w_up, w_down):
    up, down = w_up[0], w_down[0]
    width, units = up.shape
    vmem, dma = pltpu.VMEM, pltpu.SemaphoreType.DMA
    whole, anywhere = pl.BlockSpec(memory_space=pltpu.VMEM), pl.BlockSpec(memory_space=pl.ANY)
    small = jax.ShapeDtypeStruct((128, 256), BF16)
    shapes = (
        small, small,
        jax.ShapeDtypeStruct((width, units), BF16),
        jax.ShapeDtypeStruct((units, width), BF16),
    )
    found = pl.pallas_call(
        fused_kernel,
        out_shape=shapes,
        in_specs=[whole] * 4 + [anywhere] * 2,
        out_specs=(whole, whole, anywhere, anywhere),
        scratch_shapes=[
            vmem((512, width), BF16), vmem((512, width), BF16), vmem((512, width), BF16),
            vmem((4, 8, 128), F32), vmem((512, 128), F32),
            vmem((width, units), BF16), vmem((units, width), BF16),
            vmem((512, units), F32), vmem((512, units), BF16), vmem((512, units), BF16),
            vmem((2, 4, 2, 256, 256), BF16), vmem((2, 4, 2, 256, 256), BF16),
            vmem((2, 4, 2, 2, 128, 256), BF16), vmem((2, 4, 2, 128, 256), BF16),
            vmem((2, 4, 128, 256), BF16), vmem((2, 4, 128, 256), BF16),
            vmem((2, 4, 128, 256), BF16), vmem((2, 3, 128, 256), BF16),
            vmem((width, units), BF16), vmem((units, width), BF16),
            dma((2,)), dma((3,)), dma((3,)), dma((2, 15)), dma((2, 15)),
            dma((2, 4, 2)), dma((2, 4, 2)), dma((2, 4, 2)), dma((2, 4, 2)), dma((2, 4)), dma((2, 4)),
            dma((2, 3)), dma((2, 3)), dma((8,)), dma((4,)),
        ],
        compiler_params=pltpu.CompilerParams(
            collective_id=0, has_side_effects=True, vmem_limit_bytes=56 * 1024 * 1024
        ),
        cost_estimate=pl.CostEstimate(flops=12 * 512 * width * units, bytes_accessed=8 * width * units, transcendentals=512 * units),
    )(expert_ids.T, gate_values.T, tokens, grad_out, up, down)
    mixed, gtok, gup, gdown = pl.pallas_call(
        settle_kernel,
        out_shape=shapes,
        in_specs=[anywhere] * 4,
        out_specs=(anywhere,) * 4,
        scratch_shapes=[dma((18,))],
        compiler_params=pltpu.CompilerParams(vmem_limit_bytes=60 * 1024 * 1024),
    )(*found)
    return mixed, gtok, gup[None], gdown[None]


def plan_slots(routed, experts, capacity):
    flat_ids = routed.reshape(-1)
    onehot = (flat_ids[:, None] == jnp.arange(experts, dtype=jnp.int32)[None, :]).astype(jnp.int32)
    before = jnp.cumsum(onehot, axis=0) - onehot
    position = jnp.sum(before * onehot, axis=1)
    counts = jnp.sum(onehot, axis=0)
    slotting_labels = flat_ids * capacity + position
    placed = (
        slotting_labels[None, :] == jnp.arange(experts * capacity, dtype=jnp.int32)[:, None]
    ).astype(jnp.bfloat16)
    return (placed, counts)


def expert_math(rows_in, rows_grad, live_mask, up_weight, down_weight):
    preact = jnp.dot(rows_in, up_weight, preferred_element_type=jnp.float32)
    sigmoid_val = jax.nn.sigmoid(preact)
    keep = live_mask[:, None]
    hidden_units = jnp.where(keep, preact * sigmoid_val, 0.0).astype(jnp.bfloat16)
    out_part = jnp.dot(hidden_units, down_weight, preferred_element_type=jnp.float32)
    grad_hidden = lax.dot_general(
        rows_grad, down_weight, (((1,), (1,)), ((), ())), preferred_element_type=jnp.float32
    )
    slope = sigmoid_val * (1.0 + preact * (1.0 - sigmoid_val))
    gradient_before_activation = jnp.where(keep, grad_hidden * slope, 0.0).astype(jnp.bfloat16)
    grad_down_e = lax.dot_general(
        hidden_units, rows_grad, (((0,), (0,)), ((), ())), preferred_element_type=jnp.float32
    )
    grad_up_e = lax.dot_general(
        rows_in,
        gradient_before_activation,
        (((0,), (0,)), ((), ())),
        preferred_element_type=jnp.float32,
    )
    dx_part = lax.dot_general(
        gradient_before_activation,
        up_weight,
        (((1,), (1,)), ((), ())),
        preferred_element_type=jnp.float32,
    )
    return (out_part, dx_part, grad_up_e, grad_down_e)


def local(tokens, expert_ids, gate_values, grad_out, w_up, w_down):
    n_rep = lax.axis_size("rep")
    n_exp = lax.axis_size("exp")
    if (n_rep, n_exp) == (8, 4) and tokens.shape == (128, 2048) and w_up.shape[2] == 1024:
        return fused(tokens, expert_ids, gate_values, grad_out, w_up, w_down)
    tok_count, width = tokens.shape
    top_k = expert_ids.shape[1]
    pair_count = tok_count * top_k
    capacity = max(2, min(tok_count, 2 * tok_count * top_k // n_exp))
    cols = width // n_rep
    up_weight = w_up[0]
    down_weight = w_down[0]
    grad_rows = (gate_values[:, :, None] * grad_out[:, None, :].astype(jnp.float32)).astype(
        jnp.bfloat16
    )
    grad_rows = grad_rows.reshape(pair_count, width)
    placed, counts = plan_slots(expert_ids, n_exp, capacity)
    summed = placed.reshape(n_exp * capacity, tok_count, top_k).sum(axis=2)
    sent_in = jnp.dot(summed, tokens, preferred_element_type=jnp.float32).astype(jnp.bfloat16)
    sent_grad = jnp.dot(placed, grad_rows, preferred_element_type=jnp.float32).astype(jnp.bfloat16)
    count_parts = jnp.stack([counts // 16, counts % 16], axis=1).astype(jnp.bfloat16)
    got_in, got_grad, got_counts = (
        lax.all_to_all(
            sent_in.reshape(n_exp, capacity, width), "exp", split_axis=0, concat_axis=0, tiled=True
        ),
        lax.all_to_all(
            sent_grad.reshape(n_exp, capacity, width),
            "exp",
            split_axis=0,
            concat_axis=0,
            tiled=True,
        ),
        lax.all_to_all(count_parts, "exp", split_axis=0, concat_axis=0, tiled=True),
    )
    count_values = got_counts[:, 0].astype(jnp.float32) * 16.0 + got_counts[:, 1].astype(
        jnp.float32
    )
    slot_mask = jnp.arange(capacity, dtype=jnp.float32)[None, :] < count_values[:, None]
    rows_in = got_in.reshape(-1, width)
    rows_grad = got_grad.reshape(-1, width)
    live_mask = slot_mask.reshape(-1)
    out_part, dx_part, grad_up_e, grad_down_e = expert_math(
        rows_in, rows_grad, live_mask, up_weight, down_weight
    )
    total_out, total_dx = (
        lax.psum(out_part.astype(jnp.bfloat16), "rep").astype(jnp.float32),
        lax.psum(dx_part.astype(jnp.bfloat16), "rep").astype(jnp.float32),
    )
    col_start = lax.axis_index("rep") * cols
    summed_out = lax.dynamic_slice_in_dim(total_out, col_start, cols, 1)
    summed_dx = lax.dynamic_slice_in_dim(total_dx, col_start, cols, 1)
    back_out, back_dx = (
        lax.all_to_all(
            summed_out.astype(jnp.bfloat16).reshape(n_exp, capacity, cols),
            "exp",
            split_axis=0,
            concat_axis=0,
            tiled=True,
        ),
        lax.all_to_all(
            summed_dx.astype(jnp.bfloat16).reshape(n_exp, capacity, cols),
            "exp",
            split_axis=0,
            concat_axis=0,
            tiled=True,
        ),
    )
    pair_out = jnp.einsum(
        "st,sd->td",
        placed,
        back_out.reshape(n_exp * capacity, cols),
        preferred_element_type=jnp.float32,
    )
    pair_dx = jnp.einsum(
        "st,sd->td",
        placed,
        back_dx.reshape(n_exp * capacity, cols),
        preferred_element_type=jnp.float32,
    )
    mixed = jnp.sum(gate_values[:, :, None] * pair_out.reshape(tok_count, top_k, cols), axis=1)
    grad_tokens = jnp.sum(pair_dx.reshape(tok_count, top_k, cols), axis=1)
    return (
        mixed.astype(jnp.bfloat16),
        grad_tokens.astype(jnp.bfloat16),
        grad_up_e.astype(jnp.bfloat16)[None],
        grad_down_e.astype(jnp.bfloat16)[None],
    )


def solution(mesh):
    return jax.shard_map(
        local,
        mesh=mesh,
        in_specs=(
            P("exp", None),
            P("exp", None),
            P("exp", None),
            P("exp", None),
            P("exp", None, "rep"),
            P("exp", "rep", None),
        ),
        out_specs=(P("exp", "rep"), P("exp", "rep"), P("exp", None, "rep"), P("exp", "rep", None)),
        check_vma=False,
    )
```

```python
import functools

import jax
import jax.numpy as jnp
from jax import lax
from jax.experimental import pallas as pl
from jax.experimental.pallas import tpu as pltpu
from jax.sharding import PartitionSpec as P

MESH = pl.DeviceIdType.MESH
F32 = jnp.float32
BF16 = jnp.bfloat16
NN = (((1,), (0,)), ((), ()))
NT = (((1,), (1,)), ((), ()))
TN = (((0,), (0,)), ((), ()))


def dot(a, b, dims):
    return lax.dot_general(a, b, dims, preferred_element_type=F32)


def fused_kernel(
    ids, gates, tok, gout, up_hbm, down_hbm,
    mixed_out, gtok_out, gup, gdown,
    x_all, g_all, gr_all, weight_all, coef, up, down, slope, hid, gpre,
    send_a, recv_a, s_sum, recv_1, mid, recv_2, q_sum, recv_3,
    load_sem, meta_send, meta_recv, gat_send, gat_recv,
    a_send, a_recv, b_send, b_recv, t_send, t_recv, c_send, c_recv,
):
    rep, e = lax.axis_index("rep"), lax.axis_index("exp")
    z, c = lax.div(rep, 2), lax.rem(rep, 2)
    y, x = lax.div(e, 2), lax.rem(e, 2)
    xn, yn = 1 - x, 1 - y
    ex, ey, ed = y * 2 + xn, yn * 2 + x, yn * 2 + xn
    p = lax.rem(z, 2)
    to_x = {"rep": rep, "exp": ex}
    to_y = {"rep": rep, "exp": ey}
    to_d = {"rep": rep, "exp": ed}
    to_sib = {"rep": z * 2 + 1 - c, "exp": e}
    to_pair = {"rep": (z + 1 - 2 * p) * 2 + c, "exp": e}

    def at_z(d):
        zz = lax.rem(z + d, 4)
        return zz, {"rep": zz * 2 + c, "exp": e}

    def remote(src, dst, send, recv, where):
        return pltpu.make_async_remote_copy(
            src_ref=src, dst_ref=dst, send_sem=send, recv_sem=recv,
            device_id=where, device_id_type=MESH,
        )

    load_up = pltpu.make_async_copy(up_hbm, up, load_sem.at[0])
    load_down = pltpu.make_async_copy(down_hbm, down, load_sem.at[1])
    load_up.start()
    load_down.start()

    barrier = pltpu.get_barrier_semaphore()
    partners = [to_x, to_y, to_d, to_sib] + [at_z(d)[1] for d in (1, 2, 3)]
    for who in partners:
        pl.semaphore_signal(barrier, inc=1, device_id=who, device_id_type=MESH)
    pl.semaphore_wait(barrier, len(partners))

    lo, own_rows, mid_rows, pair_rows = 64 * c + 16 * p, 64 * c + 48 * p, 64 * c + 16, 64 * c + 48 - 48 * p

    def rows(block, start, count):
        return pl.ds(pl.multiple_of(block * 128 + start, 16), count)

    class Gather:
        def __init__(self, t, own, buf):
            self.t, self.own, self.buf, self.copies = t, own, buf, {}

        def send(self, k, src, block, start, count, where):
            at = rows(block, start, count)
            copy = remote(
                self.buf.at[at] if src is None else src, self.buf.at[at],
                gat_send.at[self.t, k], gat_recv.at[self.t, k], where,
            )
            copy.start()
            self.copies[k] = copy

        def direct(self):
            own_piece, mid_piece = (own_rows, 16), (mid_rows, 32)
            self.pieces = (own_piece, mid_piece) if self.t == 0 else (mid_piece, own_piece)
            first, second = self.pieces
            for k, (start, count), where in ((0, first, to_x), (1, second, to_y), (2, second, to_x), (3, first, to_y)):
                mine = self.own.at[pl.ds(pl.multiple_of(start, 16), count)]
                self.send(k, mine, e, start, count, where)

        def keep(self):
            self.buf[rows(e, 0, 128), :] = self.own[...]

        def around(self):
            first, second = self.pieces
            self.copies[0].wait_recv()
            self.send(4, None, ex, *first, to_y)
            self.copies[1].wait_recv()
            self.send(5, None, ey, *second, to_x)

        def share(self):
            self.copies[2].wait_recv()
            self.send(6, None, ex, own_rows, 16, to_pair)
            self.send(9, None, ex, lo, 48, to_sib)
            self.copies[3].wait_recv()
            self.send(7, None, ey, own_rows, 16, to_pair)
            self.send(10, None, ey, lo, 48, to_sib)

        def diagonal(self):
            self.copies[4].wait_recv()
            self.copies[5].wait_recv()
            self.send(8, None, ed, own_rows, 16, to_pair)
            self.send(11, None, ed, lo, 48, to_sib)

        def pair(self, blocks=(0, 1, 2)):
            for k in blocks:
                self.copies[6 + k].wait_recv()
                self.send(12 + k, None, (ex, ey, ed)[k], pair_rows, 16, to_sib)

        def finish(self, blocks):
            for k in blocks:
                self.copies[9 + k].wait_recv()
                self.copies[12 + k].wait_recv()

        def drain(self):
            for k in range(15):
                self.copies[k].wait_send()

    gx, gg = Gather(0, tok, x_all), Gather(1, gout, g_all)
    gx.direct()
    expert = lax.broadcasted_iota(jnp.int32, (8, 128), 0)
    first_gate = jnp.where(ids[0:1, :] == expert, gates[0:1, :], 0.0)
    weight_all[pl.ds(e, 1)] = (first_gate + jnp.where(ids[1:2, :] == expert, gates[1:2, :], 0.0))[None]
    weights = []
    for k, where in enumerate((to_x, to_y, to_d)):
        copy = remote(weight_all.at[e], weight_all.at[e], meta_send.at[k], meta_recv.at[k], where)
        copy.start()
        weights.append(copy)
    gx.keep()
    gg.keep()
    gx.around()
    gg.direct()
    gx.share()
    for copy in weights:
        copy.wait_recv()
    for block in range(4):
        line = weight_all[block, pl.ds(e, 1), :]
        coef[128 * block : 128 * block + 128, :] = jnp.broadcast_to(line, (128, 128)).T
    load_up.wait()

    def cols(n):
        return pl.ds(pl.multiple_of(n * 256, 256), 256)

    def up_tiles(yy, tiles):
        for n in tiles:
            pre = dot(x_all[cols(yy), :], up[:, cols(n)], NN)
            sig = jax.nn.sigmoid(pre)
            hid[cols(yy), cols(n)] = (pre * sig).astype(BF16)
            slope[cols(yy), cols(n)] = sig * (1.0 + pre * (1.0 - sig))

    gx.pair((0, 1))
    gx.finish((0,))
    up_tiles(y, (0, 1))
    gx.diagonal()
    gg.around()
    up_tiles(y, (2, 3))
    gx.pair((2,))
    gg.share()
    gx.finish((1, 2))
    up_tiles(yn, (0, 1, 2, 3))
    load_down.wait()

    def partial(q, yy, n):
        at = slice(None) if yy is None else cols(yy)
        if q == 0:
            scale = coef[at, :]
            return dot(hid[at, :], down[:, cols(n)], NN) * jnp.concatenate([scale, scale], axis=1)
        return dot(gpre[at, :], up[cols(n), :], NT)

    def copy_a(q, yy, zz):
        return remote(
            send_a.at[q, zz, yy], recv_a.at[q, zz, yy], a_send.at[q, zz, yy], a_recv.at[q, zz, yy], to_sib
        )

    def copy_bx(q, yy, zz):
        return remote(
            s_sum.at[q, zz, yy, xn], recv_1.at[q, zz, yy], b_send.at[q, zz, yy], b_recv.at[q, zz, yy], to_x
        )

    def copy_by(q, zz):
        return remote(s_sum.at[q, zz, yn], recv_1.at[q, zz], b_send.at[q, zz, 0], b_recv.at[q, zz, 0], to_y)

    def copy_t(q, zz):
        where = to_y if zz < 2 else to_x
        return remote(mid.at[q, zz], recv_2.at[q, zz], t_send.at[q, zz], t_recv.at[q, zz], where)

    def copy_c(q, zz, d):
        where = {"rep": zz * 2 + c, "exp": e}
        return remote(q_sum.at[q, zz], recv_3.at[q, d - 1], c_send.at[q, d - 1], c_recv.at[q, d - 1], where)

    def other_half(q, yy):
        halves = (0, 1) if yy is None else (yy,)
        for pair in ((2, 3), (0, 1)):
            for zz in pair:
                part = partial(q, yy, 2 * zz + 1 - c).astype(BF16)
                if yy is None:
                    send_a[q, zz] = part.reshape(2, 256, 256)
                else:
                    send_a[q, zz, yy] = part
            for zz in pair:
                for half in halves:
                    copy_a(q, half, zz).start()

    def own_half(q, yy, far):
        halves = (0, 1) if yy is None else (yy,)
        for pair in ((2, 3), (0, 1)):
            for zz in pair:
                for half in halves:
                    copy_a(q, half, zz).wait_recv()
            for zz in pair:
                part = partial(q, yy, 2 * zz + c)
                if yy is None:
                    total = part + recv_a[q, zz].reshape(512, 256).astype(F32)
                    s_sum[q, zz] = total.astype(BF16).reshape(2, 2, 128, 256)
                else:
                    total = part + recv_a[q, zz, yy].astype(F32)
                    s_sum[q, zz, yy] = total.astype(BF16).reshape(2, 128, 256)
            for zz in pair:
                if zz < 2:
                    for half in halves:
                        copy_bx(q, half, zz).start()
                elif far:
                    copy_by(q, zz).start()

    def second_hop(q, zs):
        for zz in zs:
            if zz < 2:
                copy_bx(q, yn, zz).wait_recv()
                mine, got = s_sum[q, zz, yn, x], recv_1[q, zz, yn]
            else:
                copy_by(q, zz).wait_recv()
                mine, got = s_sum[q, zz, y, xn], recv_1[q, zz, xn]
            mid[q, zz] = (mine.astype(F32) + got.astype(F32)).astype(BF16)
            copy_t(q, zz).start()

    def along_z(q, zs):
        for zz in zs:
            if zz < 2:
                copy_bx(q, y, zz).wait_recv()
            copy_t(q, zz).wait_recv()
            got = recv_1[q, zz, y] if zz < 2 else recv_1[q, zz, x]
            total = s_sum[q, zz, y, x].astype(F32) + got.astype(F32) + recv_2[q, zz].astype(F32)
            q_sum[q, zz] = total.astype(BF16)
            d = lax.rem(zz - z + 4, 4)

            @pl.when(d > 0)
            def _():
                copy_c(q, zz, d).start()

    def result(q, out):
        total = q_sum[q, z].astype(F32)
        for d in (1, 2, 3):
            copy_c(q, lax.rem(z + d, 4), d).wait_recv()
            total = total + recv_3[q, d - 1].astype(F32)
        out[...] = total.astype(BF16)

    def gup_tile(n, carry):
        gup[cols(n), :] = dot(x_all[:, cols(n)], gpre[...], TN).astype(BF16)
        return carry

    def gdown_tile(n, carry):
        gdown[cols(n), :] = dot(hid[:, cols(n)], gr_all[...], TN).astype(BF16)
        return carry

    other_half(0, None)
    gg.diagonal()
    gg.pair()
    own_half(0, None, True)
    gg.finish((0, 1, 2))

    def scale_half(yy):
        for n in range(16):
            at = pl.ds(n * 128, 128)
            gr_all[cols(yy), at] = (g_all[cols(yy), at].astype(F32) * coef[cols(yy), :]).astype(BF16)

    def gpre_half(yy):
        for n in range(4):
            grad = dot(gr_all[cols(yy), :], down[cols(n), :], NT)
            gpre[cols(yy), cols(n)] = (grad * slope[cols(yy), cols(n)]).astype(BF16)

    order = (2, 0, 3, 1)
    scale_half(yn)
    gpre_half(yn)
    second_hop(0, order)
    other_half(1, yn)
    own_half(1, yn, True)
    scale_half(y)
    gpre_half(y)
    along_z(0, order)
    other_half(1, y)
    second_hop(1, (0, 1))
    own_half(1, y, False)
    second_hop(1, (2, 3))
    lax.fori_loop(0, 4, gdown_tile, 0, unroll=2)
    along_z(1, (0, 2))
    lax.fori_loop(0, 2, gup_tile, 0, unroll=2)
    along_z(1, (1, 3))
    lax.fori_loop(2, 8, gup_tile, 0, unroll=2)
    result(0, mixed_out)
    result(1, gtok_out)

    gx.drain()
    gg.drain()
    for copy in weights:
        copy.wait_send()
    for q in (0, 1):
        for zz in range(4):
            for yy in (0, 1):
                copy_a(q, yy, zz).wait_send()
            if zz < 2:
                copy_bx(q, 0, zz).wait_send()
                copy_bx(q, 1, zz).wait_send()
            else:
                copy_by(q, zz).wait_send()
            copy_t(q, zz).wait_send()
        for d in (1, 2, 3):
            copy_c(q, lax.rem(z + d, 4), d).wait_send()


def settle_kernel(mixed, gtok, gup, gdown, mixed_out, gtok_out, gup_out, gdown_out, sem):
    pieces = []
    for src, dst in ((gup, gup_out), (gdown, gdown_out)):
        step = src.shape[0] // 8
        pieces += [(src.at[pl.ds(k * step, step)], dst.at[pl.ds(k * step, step)]) for k in range(8)]
    copies = [pltpu.make_async_copy(src, dst, sem.at[k]) for k, (src, dst) in enumerate(pieces)]
    for copy in copies:
        copy.start()
    mixed_out[...] = mixed[...]
    gtok_out[...] = gtok[...]
    for copy in copies:
        copy.wait()


def fused(tokens, expert_ids, gate_values, grad_out, w_up, w_down):
    up, down = w_up[0], w_down[0]
    width, units = up.shape
    vmem, dma = pltpu.VMEM, pltpu.SemaphoreType.DMA
    whole, anywhere = pl.BlockSpec(memory_space=pltpu.VMEM), pl.BlockSpec(memory_space=pl.ANY)
    small = jax.ShapeDtypeStruct((128, 256), BF16)
    shapes = (
        small, small,
        jax.ShapeDtypeStruct((width, units), BF16),
        jax.ShapeDtypeStruct((units, width), BF16),
    )
    found = pl.pallas_call(
        fused_kernel,
        out_shape=(small, small, pltpu.VMEM((width, units), BF16), pltpu.VMEM((units, width), BF16)),
        in_specs=[whole] * 4 + [anywhere] * 2,
        out_specs=(whole,) * 4,
        scratch_shapes=[
            vmem((512, width), BF16), vmem((512, width), BF16), vmem((512, width), BF16),
            vmem((4, 8, 128), F32), vmem((512, 128), F32),
            vmem((width, units), BF16), vmem((units, width), BF16),
            vmem((512, units), F32), vmem((512, units), BF16), vmem((512, units), BF16),
            vmem((2, 4, 2, 256, 256), BF16), vmem((2, 4, 2, 256, 256), BF16),
            vmem((2, 4, 2, 2, 128, 256), BF16), vmem((2, 4, 2, 128, 256), BF16),
            vmem((2, 4, 128, 256), BF16), vmem((2, 4, 128, 256), BF16),
            vmem((2, 4, 128, 256), BF16), vmem((2, 3, 128, 256), BF16),
            dma((2,)), dma((3,)), dma((3,)), dma((2, 15)), dma((2, 15)),
            dma((2, 4, 2)), dma((2, 4, 2)), dma((2, 4, 2)), dma((2, 4, 2)), dma((2, 4)), dma((2, 4)),
            dma((2, 3)), dma((2, 3)),
        ],
        compiler_params=pltpu.CompilerParams(
            collective_id=0, has_side_effects=True, vmem_limit_bytes=44 * 1024 * 1024
        ),
        cost_estimate=pl.CostEstimate(flops=12 * 512 * width * units, bytes_accessed=8 * width * units, transcendentals=512 * units),
    )(expert_ids.T, gate_values.T, tokens, grad_out, up, down)
    mixed, gtok, gup, gdown = pl.pallas_call(
        settle_kernel,
        out_shape=shapes,
        in_specs=[whole, whole, whole, whole],
        out_specs=(whole, whole, anywhere, anywhere),
        scratch_shapes=[dma((16,))],
        compiler_params=pltpu.CompilerParams(vmem_limit_bytes=16 * 1024 * 1024),
    )(*found)
    return mixed, gtok, gup[None], gdown[None]


def plan_slots(routed, experts, capacity):
    flat_ids = routed.reshape(-1)
    onehot = (flat_ids[:, None] == jnp.arange(experts, dtype=jnp.int32)[None, :]).astype(jnp.int32)
    before = jnp.cumsum(onehot, axis=0) - onehot
    position = jnp.sum(before * onehot, axis=1)
    counts = jnp.sum(onehot, axis=0)
    slotting_labels = flat_ids * capacity + position
    placed = (
        slotting_labels[None, :] == jnp.arange(experts * capacity, dtype=jnp.int32)[:, None]
    ).astype(jnp.bfloat16)
    return (placed, counts)


def expert_math(rows_in, rows_grad, live_mask, up_weight, down_weight):
    preact = jnp.dot(rows_in, up_weight, preferred_element_type=jnp.float32)
    sigmoid_val = jax.nn.sigmoid(preact)
    keep = live_mask[:, None]
    hidden_units = jnp.where(keep, preact * sigmoid_val, 0.0).astype(jnp.bfloat16)
    out_part = jnp.dot(hidden_units, down_weight, preferred_element_type=jnp.float32)
    grad_hidden = lax.dot_general(
        rows_grad, down_weight, (((1,), (1,)), ((), ())), preferred_element_type=jnp.float32
    )
    slope = sigmoid_val * (1.0 + preact * (1.0 - sigmoid_val))
    gradient_before_activation = jnp.where(keep, grad_hidden * slope, 0.0).astype(jnp.bfloat16)
    grad_down_e = lax.dot_general(
        hidden_units, rows_grad, (((0,), (0,)), ((), ())), preferred_element_type=jnp.float32
    )
    grad_up_e = lax.dot_general(
        rows_in,
        gradient_before_activation,
        (((0,), (0,)), ((), ())),
        preferred_element_type=jnp.float32,
    )
    dx_part = lax.dot_general(
        gradient_before_activation,
        up_weight,
        (((1,), (1,)), ((), ())),
        preferred_element_type=jnp.float32,
    )
    return (out_part, dx_part, grad_up_e, grad_down_e)


def local(tokens, expert_ids, gate_values, grad_out, w_up, w_down):
    n_rep = lax.axis_size("rep")
    n_exp = lax.axis_size("exp")
    if (n_rep, n_exp) == (8, 4) and tokens.shape == (128, 2048) and w_up.shape[2] == 1024:
        return fused(tokens, expert_ids, gate_values, grad_out, w_up, w_down)
    tok_count, width = tokens.shape
    top_k = expert_ids.shape[1]
    pair_count = tok_count * top_k
    capacity = max(2, min(tok_count, 2 * tok_count * top_k // n_exp))
    cols = width // n_rep
    up_weight = w_up[0]
    down_weight = w_down[0]
    grad_rows = (gate_values[:, :, None] * grad_out[:, None, :].astype(jnp.float32)).astype(
        jnp.bfloat16
    )
    grad_rows = grad_rows.reshape(pair_count, width)
    placed, counts = plan_slots(expert_ids, n_exp, capacity)
    summed = placed.reshape(n_exp * capacity, tok_count, top_k).sum(axis=2)
    sent_in = jnp.dot(summed, tokens, preferred_element_type=jnp.float32).astype(jnp.bfloat16)
    sent_grad = jnp.dot(placed, grad_rows, preferred_element_type=jnp.float32).astype(jnp.bfloat16)
    count_parts = jnp.stack([counts // 16, counts % 16], axis=1).astype(jnp.bfloat16)
    got_in, got_grad, got_counts = (
        lax.all_to_all(
            sent_in.reshape(n_exp, capacity, width), "exp", split_axis=0, concat_axis=0, tiled=True
        ),
        lax.all_to_all(
            sent_grad.reshape(n_exp, capacity, width),
            "exp",
            split_axis=0,
            concat_axis=0,
            tiled=True,
        ),
        lax.all_to_all(count_parts, "exp", split_axis=0, concat_axis=0, tiled=True),
    )
    count_values = got_counts[:, 0].astype(jnp.float32) * 16.0 + got_counts[:, 1].astype(
        jnp.float32
    )
    slot_mask = jnp.arange(capacity, dtype=jnp.float32)[None, :] < count_values[:, None]
    rows_in = got_in.reshape(-1, width)
    rows_grad = got_grad.reshape(-1, width)
    live_mask = slot_mask.reshape(-1)
    out_part, dx_part, grad_up_e, grad_down_e = expert_math(
        rows_in, rows_grad, live_mask, up_weight, down_weight
    )
    total_out, total_dx = (
        lax.psum(out_part.astype(jnp.bfloat16), "rep").astype(jnp.float32),
        lax.psum(dx_part.astype(jnp.bfloat16), "rep").astype(jnp.float32),
    )
    col_start = lax.axis_index("rep") * cols
    summed_out = lax.dynamic_slice_in_dim(total_out, col_start, cols, 1)
    summed_dx = lax.dynamic_slice_in_dim(total_dx, col_start, cols, 1)
    back_out, back_dx = (
        lax.all_to_all(
            summed_out.astype(jnp.bfloat16).reshape(n_exp, capacity, cols),
            "exp",
            split_axis=0,
            concat_axis=0,
            tiled=True,
        ),
        lax.all_to_all(
            summed_dx.astype(jnp.bfloat16).reshape(n_exp, capacity, cols),
            "exp",
            split_axis=0,
            concat_axis=0,
            tiled=True,
        ),
    )
    pair_out = jnp.einsum(
        "st,sd->td",
        placed,
        back_out.reshape(n_exp * capacity, cols),
        preferred_element_type=jnp.float32,
    )
    pair_dx = jnp.einsum(
        "st,sd->td",
        placed,
        back_dx.reshape(n_exp * capacity, cols),
        preferred_element_type=jnp.float32,
    )
    mixed = jnp.sum(gate_values[:, :, None] * pair_out.reshape(tok_count, top_k, cols), axis=1)
    grad_tokens = jnp.sum(pair_dx.reshape(tok_count, top_k, cols), axis=1)
    return (
        mixed.astype(jnp.bfloat16),
        grad_tokens.astype(jnp.bfloat16),
        grad_up_e.astype(jnp.bfloat16)[None],
        grad_down_e.astype(jnp.bfloat16)[None],
    )


def solution(mesh):
    return jax.shard_map(
        local,
        mesh=mesh,
        in_specs=(
            P("exp", None),
            P("exp", None),
            P("exp", None),
            P("exp", None),
            P("exp", None, "rep"),
            P("exp", "rep", None),
        ),
        out_specs=(P("exp", "rep"), P("exp", "rep"), P("exp", None, "rep"), P("exp", "rep", None)),
        check_vma=False,
    )
```

```python
import functools

import jax
import jax.numpy as jnp
from jax import lax
from jax.experimental import pallas as pl
from jax.experimental.pallas import tpu as pltpu
from jax.sharding import PartitionSpec as P

MESH = pl.DeviceIdType.MESH
F32 = jnp.float32
BF16 = jnp.bfloat16
NN = (((1,), (0,)), ((), ()))
NT = (((1,), (1,)), ((), ()))
TN = (((0,), (0,)), ((), ()))


def dot(a, b, dims):
    return lax.dot_general(a, b, dims, preferred_element_type=F32)


def fused_kernel(
    ids_hbm, gates_hbm, tok, gout, up_hbm, down_hbm,
    mixed_out, gtok_out, x_all, gpre, gdown,
    ids, gates, g_all, gr_all, weight_all, coef, up, down, slope, hid,
    send_a, recv_a, s_sum, recv_1, mid, recv_2, q_sum, recv_3,
    load_sem, meta_send, meta_recv, gat_send, gat_recv,
    a_send, a_recv, b_send, b_recv, t_send, t_recv, c_send, c_recv,
):
    rep, e = lax.axis_index("rep"), lax.axis_index("exp")
    z, c = lax.div(rep, 2), lax.rem(rep, 2)
    y, x = lax.div(e, 2), lax.rem(e, 2)
    xn, yn = 1 - x, 1 - y
    ex, ey, ed = y * 2 + xn, yn * 2 + x, yn * 2 + xn
    p = lax.rem(z, 2)
    to_x = {"rep": rep, "exp": ex}
    to_y = {"rep": rep, "exp": ey}
    to_d = {"rep": rep, "exp": ed}
    to_sib = {"rep": z * 2 + 1 - c, "exp": e}
    to_pair = {"rep": (z + 1 - 2 * p) * 2 + c, "exp": e}

    def at_z(d):
        zz = lax.rem(z + d, 4)
        return zz, {"rep": zz * 2 + c, "exp": e}

    def remote(src, dst, send, recv, where):
        return pltpu.make_async_remote_copy(
            src_ref=src, dst_ref=dst, send_sem=send, recv_sem=recv,
            device_id=where, device_id_type=MESH,
        )

    load_up = pltpu.make_async_copy(up_hbm, up, load_sem.at[0])
    load_down = pltpu.make_async_copy(down_hbm, down, load_sem.at[1])
    load_ids = pltpu.make_async_copy(ids_hbm, ids, load_sem.at[2])
    load_gates = pltpu.make_async_copy(gates_hbm, gates, load_sem.at[3])
    load_ids.start()
    load_gates.start()

    barrier = pltpu.get_barrier_semaphore()
    partners = [to_x, to_y, to_d, to_sib] + [at_z(d)[1] for d in (1, 2, 3)]
    for who in partners:
        pl.semaphore_signal(barrier, inc=1, device_id=who, device_id_type=MESH)
    pl.semaphore_wait(barrier, len(partners))

    lo, own_rows, mid_rows, pair_rows = 64 * c + 16 * p, 64 * c + 48 * p, 64 * c + 16, 64 * c + 48 - 48 * p

    def rows(block, start, count):
        return pl.ds(pl.multiple_of(block * 128 + start, 16), count)

    class Gather:
        def __init__(self, t, own, buf):
            self.t, self.own, self.buf, self.copies = t, own, buf, {}

        def send(self, k, src, block, start, count, where):
            at = rows(block, start, count)
            copy = remote(
                self.buf.at[at] if src is None else src, self.buf.at[at],
                gat_send.at[self.t, k], gat_recv.at[self.t, k], where,
            )
            copy.start()
            self.copies[k] = copy

        def direct(self):
            own_piece, mid_piece = (own_rows, 16), (mid_rows, 32)
            self.pieces = (own_piece, mid_piece) if self.t == 0 else (mid_piece, own_piece)
            first, second = self.pieces
            for k, (start, count), where in ((0, first, to_x), (1, second, to_y), (2, second, to_x), (3, first, to_y)):
                mine = self.own.at[pl.ds(pl.multiple_of(start, 16), count)]
                self.send(k, mine, e, start, count, where)

        def keep(self):
            self.own_copy = pltpu.make_async_copy(self.own, self.buf.at[rows(e, 0, 128)], load_sem.at[4 + self.t])
            self.own_copy.start()

        def around(self):
            first, second = self.pieces
            self.copies[0].wait_recv()
            self.send(4, None, ex, *first, to_y)
            if self.t == 0:
                self.send(6, None, ex, own_rows, 16, to_pair)
            self.copies[1].wait_recv()
            self.send(5, None, ey, *second, to_x)

        def share(self):
            self.copies[2].wait_recv()
            if self.t == 1:
                self.send(6, None, ex, own_rows, 16, to_pair)
            self.send(9, None, ex, lo, 48, to_sib)
            self.copies[3].wait_recv()
            self.send(7, None, ey, own_rows, 16, to_pair)
            self.send(10, None, ey, lo, 48, to_sib)

        def diagonal(self):
            self.copies[4 + self.t].wait_recv()
            self.send(8, None, ed, own_rows, 16, to_pair)
            self.copies[5 - self.t].wait_recv()
            self.send(11, None, ed, lo, 48, to_sib)

        def pair(self, blocks=(0, 1, 2)):
            for k in blocks:
                self.copies[6 + k].wait_recv()
                self.send(12 + k, None, (ex, ey, ed)[k], pair_rows, 16, to_sib)

        def finish(self, blocks):
            for k in blocks:
                self.copies[9 + k].wait_recv()
                self.copies[12 + k].wait_recv()

        def drain(self):
            for k in range(15):
                self.copies[k].wait_send()

    gx, gg = Gather(0, tok, x_all), Gather(1, gout, g_all)
    gx.direct()
    gx.keep()
    load_up.start()
    gg.keep()
    load_down.start()
    load_ids.wait()
    load_gates.wait()
    expert = lax.broadcasted_iota(jnp.int32, (8, 128), 0)
    first_gate = jnp.where(ids[0:1, :] == expert, gates[0:1, :], 0.0)
    weight_all[pl.ds(e, 1)] = (first_gate + jnp.where(ids[1:2, :] == expert, gates[1:2, :], 0.0))[None]
    weights = []
    for k, where in enumerate((to_x, to_y, to_d)):
        copy = remote(weight_all.at[e], weight_all.at[e], meta_send.at[k], meta_recv.at[k], where)
        copy.start()
        weights.append(copy)
    gx.around()
    gg.direct()
    gx.share()
    for copy in weights:
        copy.wait_recv()
    for block in range(4):
        line = weight_all[block, pl.ds(e, 1), :]
        coef[128 * block : 128 * block + 128, :] = jnp.broadcast_to(line, (128, 128)).T
    load_up.wait()

    def cols(n):
        return pl.ds(pl.multiple_of(n * 256, 256), 256)

    def up_tiles(yy, tiles):
        for n in tiles:
            pre = dot(x_all[cols(yy), :], up[:, cols(n)], NN)
            sig = jax.nn.sigmoid(pre)
            hid[cols(yy), cols(n)] = (pre * sig).astype(BF16)
            slope[cols(yy), cols(n)] = sig * (1.0 + pre * (1.0 - sig))

    gx.pair((0, 1))
    gx.own_copy.wait()
    gx.finish((0,))
    up_tiles(y, (0, 1))
    gx.diagonal()
    gg.around()
    up_tiles(y, (2, 3))
    gx.pair((2,))
    gg.share()
    gx.finish((1, 2))
    up_tiles(yn, (0, 1, 2, 3))
    load_down.wait()

    def partial(q, yy, n):
        at = slice(None) if yy is None else cols(yy)
        if q == 0:
            scale = coef[at, :]
            return dot(hid[at, :], down[:, cols(n)], NN) * jnp.concatenate([scale, scale], axis=1)
        return dot(gpre[at, :], up[cols(n), :], NT)

    def copy_a(q, yy, zz):
        return remote(
            send_a.at[q, zz, yy], recv_a.at[q, zz, yy], a_send.at[q, zz, yy], a_recv.at[q, zz, yy], to_sib
        )

    def copy_bx(q, yy, zz):
        return remote(
            s_sum.at[q, zz, yy, xn], recv_1.at[q, zz, yy], b_send.at[q, zz, yy], b_recv.at[q, zz, yy], to_x
        )

    def copy_by(q, zz):
        return remote(s_sum.at[q, zz, yn], recv_1.at[q, zz], b_send.at[q, zz, 0], b_recv.at[q, zz, 0], to_y)

    def copy_t(q, zz):
        where = to_y if zz < 2 else to_x
        return remote(mid.at[q, zz], recv_2.at[q, zz], t_send.at[q, zz], t_recv.at[q, zz], where)

    def copy_c(q, zz, d):
        where = {"rep": zz * 2 + c, "exp": e}
        return remote(q_sum.at[q, zz], recv_3.at[q, d - 1], c_send.at[q, d - 1], c_recv.at[q, d - 1], where)

    def other_half(q, yy):
        halves = (0, 1) if yy is None else (yy,)
        for pair in ((2, 3), (0, 1)):
            for zz in pair:
                part = partial(q, yy, 2 * zz + 1 - c).astype(BF16)
                if yy is None:
                    send_a[q, zz] = part.reshape(2, 256, 256)
                else:
                    send_a[q, zz, yy] = part
            for zz in pair:
                for half in halves:
                    copy_a(q, half, zz).start()

    def own_half(q, yy, far):
        halves = (0, 1) if yy is None else (yy,)
        for pair in ((2, 3), (0, 1)):
            for zz in pair:
                for half in halves:
                    copy_a(q, half, zz).wait_recv()
            for zz in pair:
                part = partial(q, yy, 2 * zz + c)
                if yy is None:
                    total = part + recv_a[q, zz].reshape(512, 256).astype(F32)
                    s_sum[q, zz] = total.astype(BF16).reshape(2, 2, 128, 256)
                else:
                    total = part + recv_a[q, zz, yy].astype(F32)
                    s_sum[q, zz, yy] = total.astype(BF16).reshape(2, 128, 256)
            for zz in pair:
                if zz < 2:
                    for half in halves:
                        copy_bx(q, half, zz).start()
                elif far:
                    copy_by(q, zz).start()

    def second_hop(q, zs):
        for zz in zs:
            if zz < 2:
                copy_bx(q, yn, zz).wait_recv()
                mine, got = s_sum[q, zz, yn, x], recv_1[q, zz, yn]
            else:
                copy_by(q, zz).wait_recv()
                mine, got = s_sum[q, zz, y, xn], recv_1[q, zz, xn]
            mid[q, zz] = (mine.astype(F32) + got.astype(F32)).astype(BF16)
            copy_t(q, zz).start()

    def along_z(q, zs):
        for zz in zs:
            if zz < 2:
                copy_bx(q, y, zz).wait_recv()
            copy_t(q, zz).wait_recv()
            got = recv_1[q, zz, y] if zz < 2 else recv_1[q, zz, x]
            total = s_sum[q, zz, y, x].astype(F32) + got.astype(F32) + recv_2[q, zz].astype(F32)
            q_sum[q, zz] = total.astype(BF16)
            d = lax.rem(zz - z + 4, 4)

            @pl.when(d > 0)
            def _():
                copy_c(q, zz, d).start()

    def result(q, out):
        total = q_sum[q, z].astype(F32)
        for d in (1, 2, 3):
            copy_c(q, lax.rem(z + d, 4), d).wait_recv()
            total = total + recv_3[q, d - 1].astype(F32)
        out[...] = total.astype(BF16)

    def gdown_tile(n, carry):
        gdown[cols(n), :] = dot(hid[:, cols(n)], gr_all[...], TN).astype(BF16)
        return carry

    other_half(0, None)
    gg.diagonal()
    gg.pair()
    own_half(0, None, True)
    gg.own_copy.wait()
    gg.finish((0, 1, 2))

    def scale_half(yy):
        for n in range(16):
            at = pl.ds(n * 128, 128)
            gr_all[cols(yy), at] = (g_all[cols(yy), at].astype(F32) * coef[cols(yy), :]).astype(BF16)

    def gpre_half(yy):
        for n in range(4):
            grad = dot(gr_all[cols(yy), :], down[cols(n), :], NT)
            gpre[cols(yy), cols(n)] = (grad * slope[cols(yy), cols(n)]).astype(BF16)

    order = (2, 0, 3, 1)
    scale_half(yn)
    gpre_half(yn)
    second_hop(0, order)
    other_half(1, yn)
    own_half(1, yn, True)
    scale_half(y)
    gpre_half(y)
    along_z(0, order)
    other_half(1, y)
    second_hop(1, (0, 1))
    own_half(1, y, False)
    second_hop(1, (2, 3))
    lax.fori_loop(0, 2, gdown_tile, 0, unroll=2)
    along_z(1, (0, 2))
    lax.fori_loop(2, 4, gdown_tile, 0, unroll=2)
    along_z(1, (1, 3))
    result(0, mixed_out)
    result(1, gtok_out)

    gx.drain()
    gg.drain()
    for copy in weights:
        copy.wait_send()
    for q in (0, 1):
        for zz in range(4):
            for yy in (0, 1):
                copy_a(q, yy, zz).wait_send()
            if zz < 2:
                copy_bx(q, 0, zz).wait_send()
                copy_bx(q, 1, zz).wait_send()
            else:
                copy_by(q, zz).wait_send()
            copy_t(q, zz).wait_send()
        for d in (1, 2, 3):
            copy_c(q, lax.rem(z + d, 4), d).wait_send()


def settle_kernel(mixed, gtok, x_all, gpre, gdown, mixed_out, gtok_out, gup_out, gdown_out, gup, sem):
    copies = []
    step = gdown.shape[0] // 4
    for k in range(4):
        at = pl.ds(k * step, step)
        copies.append(pltpu.make_async_copy(gdown.at[at], gdown_out.at[at], sem.at[k]))
        copies[-1].start()
    mixed_out[...] = mixed[...]
    gtok_out[...] = gtok[...]
    step = gup.shape[0] // 8
    for k in range(8):
        at = pl.ds(k * step, step)
        gup[at, :] = dot(x_all[:, at], gpre[...], TN).astype(BF16)
        copies.append(pltpu.make_async_copy(gup.at[at], gup_out.at[at], sem.at[4 + k]))
        copies[-1].start()
    for copy in copies:
        copy.wait()


def fused(tokens, expert_ids, gate_values, grad_out, w_up, w_down):
    up, down = w_up[0], w_down[0]
    width, units = up.shape
    vmem, dma = pltpu.VMEM, pltpu.SemaphoreType.DMA
    whole, anywhere = pl.BlockSpec(memory_space=pltpu.VMEM), pl.BlockSpec(memory_space=pl.ANY)
    small = jax.ShapeDtypeStruct((128, 256), BF16)
    shapes = (
        small, small,
        jax.ShapeDtypeStruct((width, units), BF16),
        jax.ShapeDtypeStruct((units, width), BF16),
    )
    found = pl.pallas_call(
        fused_kernel,
        out_shape=(
            small, small, pltpu.VMEM((512, width), BF16), pltpu.VMEM((512, units), BF16),
            pltpu.VMEM((units, width), BF16),
        ),
        in_specs=[pl.BlockSpec(memory_space=pltpu.HBM)] * 4 + [anywhere] * 2,
        out_specs=(whole,) * 5,
        scratch_shapes=[
            vmem((2, 128), jnp.int32), vmem((2, 128), F32),
            vmem((512, width), BF16), vmem((512, width), BF16),
            vmem((4, 8, 128), F32), vmem((512, 128), F32),
            vmem((width, units), BF16), vmem((units, width), BF16),
            vmem((512, units), F32), vmem((512, units), BF16),
            vmem((2, 4, 2, 256, 256), BF16), vmem((2, 4, 2, 256, 256), BF16),
            vmem((2, 4, 2, 2, 128, 256), BF16), vmem((2, 4, 2, 128, 256), BF16),
            vmem((2, 4, 128, 256), BF16), vmem((2, 4, 128, 256), BF16),
            vmem((2, 4, 128, 256), BF16), vmem((2, 3, 128, 256), BF16),
            dma((6,)), dma((3,)), dma((3,)), dma((2, 15)), dma((2, 15)),
            dma((2, 4, 2)), dma((2, 4, 2)), dma((2, 4, 2)), dma((2, 4, 2)), dma((2, 4)), dma((2, 4)),
            dma((2, 3)), dma((2, 3)),
        ],
        compiler_params=pltpu.CompilerParams(
            collective_id=0, has_side_effects=True, vmem_limit_bytes=44 * 1024 * 1024
        ),
        cost_estimate=pl.CostEstimate(flops=12 * 512 * width * units, bytes_accessed=8 * width * units, transcendentals=512 * units),
    )(*(pltpu.with_memory_space_constraint(a, pltpu.HBM) for a in (expert_ids.T, gate_values.T, tokens, grad_out)), up, down)
    mixed, gtok, gup, gdown = pl.pallas_call(
        settle_kernel,
        out_shape=shapes,
        in_specs=[whole] * 5,
        out_specs=(whole, whole, anywhere, anywhere),
        scratch_shapes=[pltpu.VMEM((width, units), BF16), dma((12,))],
        compiler_params=pltpu.CompilerParams(vmem_limit_bytes=24 * 1024 * 1024),
    )(*found)
    return mixed, gtok, gup[None], gdown[None]


def plan_slots(routed, experts, capacity):
    flat_ids = routed.reshape(-1)
    onehot = (flat_ids[:, None] == jnp.arange(experts, dtype=jnp.int32)[None, :]).astype(jnp.int32)
    before = jnp.cumsum(onehot, axis=0) - onehot
    position = jnp.sum(before * onehot, axis=1)
    counts = jnp.sum(onehot, axis=0)
    slotting_labels = flat_ids * capacity + position
    placed = (
        slotting_labels[None, :] == jnp.arange(experts * capacity, dtype=jnp.int32)[:, None]
    ).astype(jnp.bfloat16)
    return (placed, counts)


def expert_math(rows_in, rows_grad, live_mask, up_weight, down_weight):
    preact = jnp.dot(rows_in, up_weight, preferred_element_type=jnp.float32)
    sigmoid_val = jax.nn.sigmoid(preact)
    keep = live_mask[:, None]
    hidden_units = jnp.where(keep, preact * sigmoid_val, 0.0).astype(jnp.bfloat16)
    out_part = jnp.dot(hidden_units, down_weight, preferred_element_type=jnp.float32)
    grad_hidden = lax.dot_general(
        rows_grad, down_weight, (((1,), (1,)), ((), ())), preferred_element_type=jnp.float32
    )
    slope = sigmoid_val * (1.0 + preact * (1.0 - sigmoid_val))
    gradient_before_activation = jnp.where(keep, grad_hidden * slope, 0.0).astype(jnp.bfloat16)
    grad_down_e = lax.dot_general(
        hidden_units, rows_grad, (((0,), (0,)), ((), ())), preferred_element_type=jnp.float32
    )
    grad_up_e = lax.dot_general(
        rows_in,
        gradient_before_activation,
        (((0,), (0,)), ((), ())),
        preferred_element_type=jnp.float32,
    )
    dx_part = lax.dot_general(
        gradient_before_activation,
        up_weight,
        (((1,), (1,)), ((), ())),
        preferred_element_type=jnp.float32,
    )
    return (out_part, dx_part, grad_up_e, grad_down_e)


def local(tokens, expert_ids, gate_values, grad_out, w_up, w_down):
    n_rep = lax.axis_size("rep")
    n_exp = lax.axis_size("exp")
    if (n_rep, n_exp) == (8, 4) and tokens.shape == (128, 2048) and w_up.shape[2] == 1024:
        return fused(tokens, expert_ids, gate_values, grad_out, w_up, w_down)
    tok_count, width = tokens.shape
    top_k = expert_ids.shape[1]
    pair_count = tok_count * top_k
    capacity = max(2, min(tok_count, 2 * tok_count * top_k // n_exp))
    cols = width // n_rep
    up_weight = w_up[0]
    down_weight = w_down[0]
    grad_rows = (gate_values[:, :, None] * grad_out[:, None, :].astype(jnp.float32)).astype(
        jnp.bfloat16
    )
    grad_rows = grad_rows.reshape(pair_count, width)
    placed, counts = plan_slots(expert_ids, n_exp, capacity)
    summed = placed.reshape(n_exp * capacity, tok_count, top_k).sum(axis=2)
    sent_in = jnp.dot(summed, tokens, preferred_element_type=jnp.float32).astype(jnp.bfloat16)
    sent_grad = jnp.dot(placed, grad_rows, preferred_element_type=jnp.float32).astype(jnp.bfloat16)
    count_parts = jnp.stack([counts // 16, counts % 16], axis=1).astype(jnp.bfloat16)
    got_in, got_grad, got_counts = (
        lax.all_to_all(
            sent_in.reshape(n_exp, capacity, width), "exp", split_axis=0, concat_axis=0, tiled=True
        ),
        lax.all_to_all(
            sent_grad.reshape(n_exp, capacity, width),
            "exp",
            split_axis=0,
            concat_axis=0,
            tiled=True,
        ),
        lax.all_to_all(count_parts, "exp", split_axis=0, concat_axis=0, tiled=True),
    )
    count_values = got_counts[:, 0].astype(jnp.float32) * 16.0 + got_counts[:, 1].astype(
        jnp.float32
    )
    slot_mask = jnp.arange(capacity, dtype=jnp.float32)[None, :] < count_values[:, None]
    rows_in = got_in.reshape(-1, width)
    rows_grad = got_grad.reshape(-1, width)
    live_mask = slot_mask.reshape(-1)
    out_part, dx_part, grad_up_e, grad_down_e = expert_math(
        rows_in, rows_grad, live_mask, up_weight, down_weight
    )
    total_out, total_dx = (
        lax.psum(out_part.astype(jnp.bfloat16), "rep").astype(jnp.float32),
        lax.psum(dx_part.astype(jnp.bfloat16), "rep").astype(jnp.float32),
    )
    col_start = lax.axis_index("rep") * cols
    summed_out = lax.dynamic_slice_in_dim(total_out, col_start, cols, 1)
    summed_dx = lax.dynamic_slice_in_dim(total_dx, col_start, cols, 1)
    back_out, back_dx = (
        lax.all_to_all(
            summed_out.astype(jnp.bfloat16).reshape(n_exp, capacity, cols),
            "exp",
            split_axis=0,
            concat_axis=0,
            tiled=True,
        ),
        lax.all_to_all(
            summed_dx.astype(jnp.bfloat16).reshape(n_exp, capacity, cols),
            "exp",
            split_axis=0,
            concat_axis=0,
            tiled=True,
        ),
    )
    pair_out = jnp.einsum(
        "st,sd->td",
        placed,
        back_out.reshape(n_exp * capacity, cols),
        preferred_element_type=jnp.float32,
    )
    pair_dx = jnp.einsum(
        "st,sd->td",
        placed,
        back_dx.reshape(n_exp * capacity, cols),
        preferred_element_type=jnp.float32,
    )
    mixed = jnp.sum(gate_values[:, :, None] * pair_out.reshape(tok_count, top_k, cols), axis=1)
    grad_tokens = jnp.sum(pair_dx.reshape(tok_count, top_k, cols), axis=1)
    return (
        mixed.astype(jnp.bfloat16),
        grad_tokens.astype(jnp.bfloat16),
        grad_up_e.astype(jnp.bfloat16)[None],
        grad_down_e.astype(jnp.bfloat16)[None],
    )


def solution(mesh):
    return jax.shard_map(
        local,
        mesh=mesh,
        in_specs=(
            P("exp", None),
            P("exp", None),
            P("exp", None),
            P("exp", None),
            P("exp", None, "rep"),
            P("exp", "rep", None),
        ),
        out_specs=(P("exp", "rep"), P("exp", "rep"), P("exp", None, "rep"), P("exp", "rep", None)),
        check_vma=False,
    )
```
